32 devices in a mesh: ctx: 8 (over z, x), head: 4 (over y, core).
Axes of the slice: x: 2, y: 2, z: 4, core: 2. Of those that a mesh axis runs over, the one named last changes fastest.
Arguments:
- queries: bfloat16 [2048, 2048], P('ctx', 'head'), may hold values from -4.5 to 4.5
- key_states: bfloat16 [2048, 512], P('ctx', 'head'), may hold values from -4.5 to 4.5
- value_states: bfloat16 [2048, 512], P('ctx', 'head'), may hold values from -6 to 6
- doc_lengths: int32 [4], replicated, may hold values from 1 to 1024, 2048 in all
- out_weight: bfloat16 [4096, 2048], P('ctx', 'head'), may hold values from -0.125 to 0.125
- out_grad: bfloat16 [2048, 4096], P('ctx', 'head'), may hold values from -6 to 6
Outputs:
- projected: bfloat16 [2048, 4096], P('ctx', 'head')
- query_grad: bfloat16 [2048, 2048], P('ctx', 'head')
- key_grad: bfloat16 [2048, 512], P('ctx', 'head')
- value_grad: bfloat16 [2048, 512], P('ctx', 'head')
The draws below stay inside these ranges and needn't reach their ends.
Inputs may be any that keep to these rules, and one draw needn't show every extreme that they name: `doc_lengths`: the lengths sum to 2048; the longest is exactly 1024.
All inputs are finite; a program needn't handle non-finite values.
Results may differ from the reference program's by a relative error of at most 0.014.
Values may be sent and summed in bfloat16 or wider, within the bound.
A program may use at most 64 MiB of HBM per device.

```python
import math
import jax
import jax.numpy as jnp
import numpy as np
from jax import lax

D = 4096
Q_HEADS = 16
KV_HEADS = 4
HEAD_DIM = 128
REACH = 4
TOK_DEV = 256
TOKENS = 2048
DOCS = 4
MOST = 1024
N_CTX = 8
N_HEAD = 4


def aligned_part(key, factor):
    signs = jnp.where(jax.random.bernoulli(key, 0.5, (TOKENS, KV_HEADS, HEAD_DIM)), 1.0, -1.0)
    positions = jnp.arange(TOKENS)
    levels = 3.2 + 0.55 * (positions // 512 % 3)
    strength = jnp.where(positions % 512 == 511, levels, 0.0) * factor
    return (signs * strength[:, None, None], strength)


def draw_queries(key, part):
    shape = (TOKENS, KV_HEADS, Q_HEADS // KV_HEADS, HEAD_DIM)
    shared, strength = aligned_part(key, 0.5)
    base = jnp.clip(jax.random.normal(jax.random.fold_in(key, 11), shape, jnp.float32), -4.5, 4.5)
    picked = strength[:, None, None, None] > 0.0
    full = jnp.where(picked, shared[:, :, None, :], base)
    return full.reshape(TOKENS, Q_HEADS * HEAD_DIM).astype(jnp.bfloat16)


def draw_key_states(key, part):
    shape = (TOKENS, KV_HEADS, HEAD_DIM)
    shared, strength = aligned_part(key, 0.5)
    base = jnp.clip(jax.random.normal(jax.random.fold_in(key, 23), shape, jnp.float32), -4.5, 4.5)
    following = jnp.roll(shared, -1, axis=0) * 0.99
    next_strength = jnp.roll(strength, -1)
    full = jnp.where(strength[:, None, None] > 0.0, shared, jnp.where(next_strength[:, None, None] > 0.0, following, base))
    return full.reshape(TOKENS, KV_HEADS * HEAD_DIM).astype(jnp.bfloat16)


def block_levels(stream_key, dims, shards, smallest, top_value):
    level, own = 1.0, jax.random.fold_in(stream_key, 6)
    for position, parts in shards:
        heights = jnp.exp(jax.random.uniform(jax.random.fold_in(own, position), (parts,), jnp.float32, smallest / len(shards), top_value / len(shards)))
        level = level * jnp.repeat(heights, dims[position] // parts).reshape([-1 if axis == position else 1 for axis in range(len(dims))])
    return level


def split_up(number_of, total, limit, slope):
    loads = [(1 << 20) // math.isqrt(standing ** slope) + 1 for standing in range(2, number_of + 1)]
    spare, counts = total - limit - (number_of - 1), [1] * (number_of - 1)
    while spare > 0:
        free = [i for i in range(number_of - 1) if counts[i] < limit]
        mass, left = sum([loads[i] for i in free]), spare
        for i in free:
            more = min(limit - counts[i], max(1, left * loads[i] // mass), spare)
            counts[i] = counts[i] + more
            spare = spare - more
    return np.array([limit] + counts)


def ragged_sizes(rng, amount, total, reach, slope):
    if amount == 2:
        one = jax.random.randint(rng, (), max(1, total - reach), min(reach, total - 1) + 1)
        return jnp.stack([one, total - one])
    sizes = jnp.asarray(split_up(amount, total, reach, slope), jnp.int32)
    pairs = (amount - 1) // 2
    giver, receiver = sizes[1:1 + 2 * pairs:2], sizes[2:2 + 2 * pairs:2]
    room = jnp.minimum(giver - 1, reach - receiver)
    shifted = jax.random.randint(jax.random.fold_in(rng, 1), (pairs,), 0, 1 << 20) % (room + 1)
    sizes = sizes.at[1:1 + 2 * pairs:2].set(giver - shifted).at[2:2 + 2 * pairs:2].set(receiver + shifted)
    return sizes[jax.random.permutation(jax.random.fold_in(rng, 2), amount)]


def scatter_about(stream_key, extent, deviation, most, split=(), kind=jnp.bfloat16):
    gain = block_levels(stream_key, extent, split, -0.22, 0.18) if split else 1.0
    array = jax.random.normal(stream_key, extent, jnp.float32) * deviation * gain
    return jnp.minimum(jnp.maximum(array, -most), most).astype(kind)


def setup_inputs(seed: int = 0) -> dict:
    key_list = jax.random.split(jax.random.key(seed), 7)
    return {
        "queries": draw_queries(jax.random.fold_in(key_list[6], 71), 0),
        "key_states": draw_key_states(jax.random.fold_in(key_list[6], 71), 0),
        "value_states": scatter_about(key_list[2], (TOKENS, KV_HEADS * HEAD_DIM), 1.0, 6.0, ((0, 8), (1, 4))),
        "doc_lengths": ragged_sizes(key_list[3], DOCS, TOKENS, MOST, 2).astype(jnp.int32),
        "out_weight": scatter_about(key_list[4], (D, Q_HEADS * HEAD_DIM), (Q_HEADS * HEAD_DIM) ** -0.5, 0.125, ((0, 8), (1, 4))),
        "out_grad": scatter_about(key_list[5], (TOKENS, D), 1.0, 6.0, ((0, 8), (1, 4))),
    }


NEGATIVE = -1e30


def doc_starts(doc_lengths, positions):
    doc_ends = jnp.cumsum(doc_lengths)
    passed = doc_ends[None, :] <= positions[:, None]
    return jnp.sum(jnp.where(passed, doc_lengths[None, :], 0), axis=1).astype(jnp.int32)


def rounded(values):
    return lax.optimization_barrier(values.astype(jnp.bfloat16)).astype(jnp.float32)


def reference(queries, key_states, value_states, doc_lengths, out_weight, out_grad):
    group_size = Q_HEADS // KV_HEADS
    score_scale = HEAD_DIM ** -0.5
    window_len = (REACH + 1) * TOK_DEV
    pad_rows = REACH * TOK_DEV
    kv_cols = KV_HEADS * HEAD_DIM
    key_pad = jnp.concatenate([jnp.zeros((pad_rows, kv_cols), jnp.bfloat16), key_states], axis=0)
    value_pad = jnp.concatenate([jnp.zeros((pad_rows, kv_cols), jnp.bfloat16), value_states], axis=0)
    positions = jnp.arange(TOKENS, dtype=jnp.int32)
    starts = doc_starts(doc_lengths, positions)
    block_ids = jnp.arange(N_CTX, dtype=jnp.int32)

    def window(block_index):
        first_row = (block_index * TOK_DEV).astype(jnp.int32)
        query_rows = lax.dynamic_slice_in_dim(queries, first_row, TOK_DEV, 0).astype(jnp.float32)
        query_rows = query_rows.reshape(TOK_DEV, KV_HEADS, group_size, HEAD_DIM)
        key_rows = lax.dynamic_slice_in_dim(key_pad, first_row, window_len, 0).astype(jnp.float32)
        key_rows = key_rows.reshape(window_len, KV_HEADS, HEAD_DIM)
        value_rows = lax.dynamic_slice_in_dim(value_pad, first_row, window_len, 0).astype(jnp.float32)
        value_rows = value_rows.reshape(window_len, KV_HEADS, HEAD_DIM)
        query_pos = first_row + jnp.arange(TOK_DEV, dtype=jnp.int32)
        key_pos = first_row - pad_rows + jnp.arange(window_len, dtype=jnp.int32)
        query_start = lax.dynamic_slice_in_dim(starts, first_row, TOK_DEV, 0)
        allowed = (key_pos[None, :] >= query_start[:, None]) & (key_pos[None, :] <= query_pos[:, None])
        scores = jnp.einsum('tgqd,cgd->gqtc', query_rows, key_rows) * score_scale
        masked = jnp.where(allowed, scores, NEGATIVE)
        return query_rows, key_rows, value_rows, allowed, masked

    def forward(block_index):
        _, _, value_rows, allowed, masked = window(block_index)
        row_max = jnp.max(masked, axis=-1, keepdims=True)
        row_sum = jnp.sum(jnp.where(allowed, jnp.exp(masked - row_max), 0.0), axis=-1, keepdims=True)
        log_rows = row_max + jnp.log(row_sum)
        soft_probs = rounded(jnp.exp(masked - log_rows))
        mixed = jnp.einsum('gqtc,cgd->tgqd', soft_probs, value_rows)
        return mixed.astype(jnp.bfloat16).reshape(TOK_DEV, Q_HEADS * HEAD_DIM), log_rows[..., 0]

    attended, log_total = lax.map(forward, block_ids)
    attended = attended.reshape(TOKENS, Q_HEADS * HEAD_DIM)

    group_cols = Q_HEADS * HEAD_DIM // N_HEAD
    summed = jnp.zeros((TOKENS, D), jnp.float32)
    for group_index in range(N_HEAD):
        lower = group_index * group_cols
        term = jnp.dot(attended[:, lower:lower + group_cols], out_weight[:, lower:lower + group_cols].T,
                       preferred_element_type=jnp.float32)
        summed = summed + rounded(term)
    projected = summed.astype(jnp.bfloat16)

    attended_grad = jnp.dot(out_grad, out_weight, preferred_element_type=jnp.float32).astype(jnp.bfloat16)
    product = attended_grad.astype(jnp.float32) * attended.astype(jnp.float32)
    row_delta = jnp.sum(product.reshape(TOKENS, KV_HEADS, group_size, HEAD_DIM), axis=-1)

    def backward(carried, block_index):
        key_acc, value_acc = carried
        query_rows, key_rows, value_rows, allowed, masked = window(block_index)
        first_row = (block_index * TOK_DEV).astype(jnp.int32)
        log_rows = log_total[block_index]
        grad_rows = lax.dynamic_slice_in_dim(attended_grad, first_row, TOK_DEV, 0).astype(jnp.float32)
        grad_rows = grad_rows.reshape(TOK_DEV, KV_HEADS, group_size, HEAD_DIM)
        delta_rows = lax.dynamic_slice_in_dim(row_delta, first_row, TOK_DEV, 0).transpose(1, 2, 0)
        exact_probs = jnp.exp(masked - log_rows[..., None])
        soft_probs = rounded(exact_probs)
        grad_probs = jnp.einsum('tgqd,cgd->gqtc', grad_rows, value_rows)
        grad_scores = rounded(exact_probs * (grad_probs - delta_rows[..., None]))
        query_part = jnp.einsum('gqtc,cgd->tgqd', grad_scores, key_rows) * score_scale
        key_part = jnp.einsum('gqtc,tgqd->cgd', grad_scores, query_rows).reshape(window_len, kv_cols)
        value_part = jnp.einsum('gqtc,tgqd->cgd', soft_probs, grad_rows).reshape(window_len, kv_cols)
        key_acc = lax.dynamic_update_slice_in_dim(
            key_acc, lax.dynamic_slice_in_dim(key_acc, first_row, window_len, 0) + key_part, first_row, 0)
        value_acc = lax.dynamic_update_slice_in_dim(
            value_acc, lax.dynamic_slice_in_dim(value_acc, first_row, window_len, 0) + value_part, first_row, 0)
        return (key_acc, value_acc), query_part.astype(jnp.bfloat16).reshape(TOK_DEV, Q_HEADS * HEAD_DIM)

    start_acc = (jnp.zeros((TOKENS + pad_rows, kv_cols), jnp.float32),
                 jnp.zeros((TOKENS + pad_rows, kv_cols), jnp.float32))
    (key_acc, value_acc), query_grad = lax.scan(backward, start_acc, block_ids)
    query_grad = query_grad.reshape(TOKENS, Q_HEADS * HEAD_DIM)
    key_grad = (key_acc[pad_rows:] * score_scale).astype(jnp.bfloat16)
    value_grad = value_acc[pad_rows:].astype(jnp.bfloat16)
    return projected, query_grad, key_grad, value_grad
```

```python
import functools

import jax
import jax.numpy as jnp
from jax import lax
from jax.experimental import pallas as pl
from jax.experimental.pallas import tpu as pltpu
from jax.sharding import PartitionSpec as P

HEAD_DIM = 128
REACH = 4
NEGATIVE = -1e30
MESH = pl.DeviceIdType.MESH
F32 = jnp.float32
BF16 = jnp.bfloat16


def dot_nn(left, right):
    return jnp.dot(left, right, preferred_element_type=F32)


def dot_nt(left, right):
    return lax.dot_general(left, right, (((1,), (1,)), ((), ())), preferred_element_type=F32)


def loop(first, last, body, carried):
    if last - first > 8:
        return lax.fori_loop(first, last, body, carried)
    for index in range(first, last):
        carried = body(index, carried)
    return carried


def flip(value):
    return value.astype(F32).T.astype(BF16)


def kernel(
    n_ctx, n_head, pieces,
    doc_ref, q_ref, k_ref, v_ref, w_ref, g_ref,
    proj_ref, qg_ref, kg_ref, vg_ref,
    kv, kv_t, q_st, probs, probs_b, att, att_t, w_all, g_all, d_acc, d_st, d_t,
    delta, ds_b, dq_t, term, term_in, kv_out, kv_in, kv_acc,
    kv_send, kv_recv, w_send, w_recv, w_own, g_send, g_recv, g_own, t_send, t_recv, b_send, b_recv,
):
    rows = q_ref.shape[0]
    heads = q_ref.shape[1] // HEAD_DIM
    w_rows = w_ref.shape[0]
    cols = g_ref.shape[1]
    chain = n_ctx // 2
    scale = HEAD_DIM ** (-0.5)
    rank = lax.axis_index("ctx")
    mine = lax.axis_index("head")
    place = rank // 2
    side = rank % 2
    other = 1 - side
    core = mine % 2
    half = mine // 2
    mate = half * 2 + (1 - core)
    across = (1 - half) * 2 + core
    diagonal = (1 - half) * 2 + (1 - core)

    barrier = pltpu.get_barrier_semaphore()
    for target in (mate, across, diagonal):
        pl.semaphore_signal(barrier, inc=1, device_id=(rank, target), device_id_type=MESH)
    for step in range(1, REACH + 1):

        @pl.when(rank - step >= 0)
        def _(step=step):
            pl.semaphore_signal(barrier, inc=1, device_id=(rank - step, mine), device_id_type=MESH)

        @pl.when(rank + step < n_ctx)
        def _(step=step):
            pl.semaphore_signal(barrier, inc=1, device_id=(rank + step, mine), device_id_type=MESH)

    below_me = jnp.where(rank < REACH, rank, REACH)
    above_me = jnp.where(n_ctx - 1 - rank < REACH, n_ctx - 1 - rank, REACH)
    pl.semaphore_wait(barrier, n_head - 1 + below_me + above_me)

    def kv_copy(step, which):
        return pltpu.make_async_remote_copy(
            src_ref=(k_ref, v_ref)[which],
            dst_ref=kv.at[which, step],
            send_sem=kv_send.at[which, step],
            recv_sem=kv_recv.at[which, step],
            device_id=(rank + step, mine),
            device_id_type=MESH,
        )

    def w_slot(chunk, piece):
        first, count = pieces[piece]
        return w_all.at[pl.ds(pl.multiple_of(chunk * w_rows + first, 16), count), :]

    def w_copy(way, chunk, piece, own=False):
        first, count = pieces[piece]
        target = (rank + 2, rank - 2, place * 2 + other)[way]
        return pltpu.make_async_remote_copy(
            src_ref=w_ref.at[pl.ds(first, count), :] if own else w_slot(chunk, piece),
            dst_ref=w_slot(chunk, piece),
            send_sem=w_send.at[way, piece, chunk],
            recv_sem=w_recv.at[piece, chunk],
            device_id=(target, mine),
            device_id_type=MESH,
        )

    def g_copy(way):
        source, target = ((mine, mate), (mine, across), (across, mate))[way]
        return pltpu.make_async_remote_copy(
            src_ref=g_all.at[source] if way == 2 else g_ref,
            dst_ref=g_all.at[source],
            send_sem=g_send.at[way],
            recv_sem=g_recv.at[source],
            device_id=(rank, target),
            device_id_type=MESH,
        )

    def g_arrival(source):
        return pltpu.make_async_remote_copy(
            src_ref=g_ref,
            dst_ref=g_all.at[source],
            send_sem=g_send.at[0],
            recv_sem=g_recv.at[source],
            device_id=(rank, mate),
            device_id_type=MESH,
        )

    def term_copy(target):
        return pltpu.make_async_remote_copy(
            src_ref=term.at[target],
            dst_ref=term_in.at[mine],
            send_sem=t_send.at[target],
            recv_sem=t_recv.at[mine],
            device_id=(rank, target),
            device_id_type=MESH,
        )

    def term_arrival(source):
        return pltpu.make_async_remote_copy(
            src_ref=term.at[source],
            dst_ref=term_in.at[source],
            send_sem=t_send.at[source],
            recv_sem=t_recv.at[source],
            device_id=(rank, mate),
            device_id_type=MESH,
        )

    def back_copy(step):
        return pltpu.make_async_remote_copy(
            src_ref=kv_out.at[step],
            dst_ref=kv_in.at[step],
            send_sem=b_send.at[step],
            recv_sem=b_recv.at[step],
            device_id=(rank - step, mine),
            device_id_type=MESH,
        )

    piece_ids = range(len(pieces))

    def own_sends(act):
        for piece in piece_ids:

            @pl.when(place + 1 < chain)
            def _(piece=piece):
                act(w_copy(0, rank, piece, own=True))

            @pl.when(place >= 1)
            def _(piece=piece):
                act(w_copy(1, rank, piece, own=True))

            act(w_copy(2, rank, piece, own=True))

    for step in range(1, REACH + 1):

        @pl.when(rank + step < n_ctx)
        def _(step=step):
            kv_copy(step, 0).start()
            kv_copy(step, 1).start()

    own_sends(lambda copy: copy.start())
    g_copy(1).start()
    g_copy(0).start()
    own_rows = w_all.at[pl.ds(pl.multiple_of(rank * w_rows, 16), w_rows), :]
    w_local = pltpu.make_async_copy(w_ref, own_rows, w_own)
    w_local.start()
    g_local = pltpu.make_async_copy(g_ref, g_all.at[mine], g_own)
    g_local.start()

    lanes = [pl.ds(head * rows, rows) for head in range(heads)]
    for head in range(heads):
        q_st[lanes[head], :] = q_ref[:, head * HEAD_DIM:(head + 1) * HEAD_DIM]
    kv[0, 0] = k_ref[...]
    kv[1, 0] = v_ref[...]

    positions = rank * rows + lax.broadcasted_iota(jnp.int32, (1, rows), 1)

    def add_doc(index, carried):
        end, starts = carried
        length = doc_ref[index]
        end = end + length
        return end, starts + jnp.where(end <= positions, length, 0)

    _, starts = loop(
        0, doc_ref.shape[0], add_doc, (jnp.int32(0), jnp.zeros((1, rows), jnp.int32))
    )

    def score_block(step, maxima):
        @pl.when(jnp.logical_and(step > 0, rank - step >= 0))
        def _():
            for which in range(2):
                pltpu.make_async_remote_copy(
                    src_ref=(k_ref, v_ref)[which],
                    dst_ref=kv.at[which, step],
                    send_sem=kv_send.at[which, step],
                    recv_sem=kv_recv.at[which, step],
                    device_id=(rank, mate),
                    device_id_type=MESH,
                ).wait_recv()

        @pl.when(rank - step < 0)
        def _():
            kv[0, step] = jnp.zeros((rows, HEAD_DIM), BF16)
            kv[1, step] = jnp.zeros((rows, HEAD_DIM), BF16)

        key_block = kv[0, step]
        kv_t[0, step] = flip(key_block)
        kv_t[1, step] = flip(kv[1, step])
        key_pos = (rank - step) * rows + lax.broadcasted_iota(jnp.int32, (rows, rows), 0)
        allowed = jnp.logical_and(key_pos >= starts, key_pos <= positions)
        result = []
        for head in range(heads):
            scores = dot_nt(key_block, q_st[lanes[head], :]) * scale
            scores = jnp.where(allowed, scores, NEGATIVE)
            probs[step, :, lanes[head]] = scores
            result.append(jnp.maximum(maxima[head], jnp.max(scores, axis=0, keepdims=True)))
        return tuple(result)

    low = jnp.full((1, rows), NEGATIVE, F32)
    maxima = loop(0, REACH + 1, score_block, (low,) * heads)

    def exp_block(step, sums):
        result = []
        for head in range(heads):
            powers = jnp.exp(probs[step, :, lanes[head]] - maxima[head])
            probs[step, :, lanes[head]] = powers
            result.append(sums[head] + jnp.sum(powers, axis=0, keepdims=True))
        return tuple(result)

    zero = jnp.zeros((1, rows), F32)
    sums = loop(0, REACH + 1, exp_block, (zero,) * heads)
    inverses = [1.0 / total for total in sums]
    dq_t[...] = jnp.zeros_like(dq_t)

    def mix_block(step, carried):
        for head in range(heads):
            exact = probs[step, :, lanes[head]] * inverses[head]
            probs[step, :, lanes[head]] = exact
            probs_b[step, :, lanes[head]] = exact.astype(BF16)
        dq_t[...] += dot_nn(kv_t[1, step], probs_b[step])
        return carried

    loop(0, REACH + 1, mix_block, 0)
    for head in range(heads):
        mixed = dq_t[:, lanes[head]]
        att_t[:, lanes[head]] = mixed.astype(BF16)
        att[:, head * HEAD_DIM:(head + 1) * HEAD_DIM] = mixed.T.astype(BF16)

    w_local.wait()
    g_local.wait()
    g_arrival(across).wait_recv()
    g_copy(2).start()
    g_arrival(mate).wait_recv()
    g_arrival(diagonal).wait_recv()
    d_acc[...] = jnp.zeros_like(d_acc)

    def process(block):
        w_block = w_all[pl.ds(pl.multiple_of(block * cols, cols), cols), :]
        d_acc[...] += dot_nn(g_all[block], w_block)
        term[block] = dot_nt(att[...], w_block).astype(BF16)

        @pl.when(block != mine)
        def _():
            term_copy(block).start()

    def x_wait(chunk):
        for piece in piece_ids:
            w_copy(2, chunk, piece).wait_recv()

    early = 2 * w_rows == cols

    def finish(step):
        def one(which, carried):
            spot = place + (2 * which - 1) * step

            @pl.when(jnp.logical_and(spot >= 0, spot < chain) & (which + step > 0))
            def _():
                x_wait(spot * 2 + other)
                if early:
                    process(spot)

            return carried

        loop(0, 2, one, 0)

    def hop(step, carried):
        below = place - step
        above = place + step
        for piece in piece_ids:

            @pl.when(below >= 0)
            def _(piece=piece):
                chunk = below * 2 + side
                w_copy(0, chunk, piece).wait_recv()

                @pl.when(place + 1 < chain)
                def _():
                    w_copy(0, chunk, piece).start()

                w_copy(2, chunk, piece).start()

            @pl.when(above < chain)
            def _(piece=piece):
                chunk = above * 2 + side
                w_copy(1, chunk, piece).wait_recv()

                @pl.when(place >= 1)
                def _():
                    w_copy(1, chunk, piece).start()

                w_copy(2, chunk, piece).start()

        finish(step - 1)
        return carried

    loop(1, chain, hop, 0)
    finish(chain - 1)
    if not early:

        def late(block, carried):
            process(block)
            return carried

        loop(0, n_head, late, 0)

    for head in range(heads):
        part = d_acc[:, head * HEAD_DIM:(head + 1) * HEAD_DIM].astype(BF16)
        d_st[lanes[head], :] = part
        turned = part.astype(F32).T
        delta[:, lanes[head]] = jnp.sum(
            turned * att_t[:, lanes[head]].astype(F32), axis=0, keepdims=True
        )
    dq_t[...] = jnp.zeros_like(dq_t)

    def grad_block(index, carried):
        step = REACH - index
        value_block = kv[1, step]
        for head in range(heads):
            d_probs = dot_nt(value_block, d_st[lanes[head], :])
            d_scores = probs[step, :, lanes[head]] * (d_probs - delta[:, lanes[head]])
            ds_b[:, lanes[head]] = d_scores.astype(BF16)
        key_part = dot_nn(ds_b[...], q_st[...])
        value_part = dot_nn(probs_b[step], d_st[...])

        @pl.when(step == 0)
        def _():
            kv_acc[0] = key_part
            kv_acc[1] = value_part

        @pl.when(jnp.logical_and(step > 0, rank - step >= 0))
        def _():
            kv_out[step, 0] = key_part.astype(BF16)
            kv_out[step, 1] = value_part.astype(BF16)
            back_copy(step).start()

        dq_t[...] += dot_nn(kv_t[0, step], ds_b[...])
        return carried

    loop(0, REACH + 1, grad_block, 0)
    for head in range(heads):
        qg_ref[:, head * HEAD_DIM:(head + 1) * HEAD_DIM] = (
            (dq_t[:, lanes[head]] * scale).T.astype(BF16)
        )

    for source in (mate, across, diagonal):
        term_arrival(source).wait_recv()
    summed = term[mine].astype(F32)
    for source in (mate, across, diagonal):
        summed = summed + term_in[source].astype(F32)
    proj_ref[...] = summed.astype(BF16)

    for step in range(REACH, 0, -1):

        @pl.when(rank + step < n_ctx)
        def _(step=step):
            back_copy(step).wait_recv()
            kv_acc[...] += kv_in[step].astype(F32)

    kg_ref[...] = (kv_acc[0] * scale).astype(BF16)
    vg_ref[...] = kv_acc[1].astype(BF16)

    for step in range(1, REACH + 1):

        @pl.when(rank + step < n_ctx)
        def _(step=step):
            kv_copy(step, 0).wait_send()
            kv_copy(step, 1).wait_send()

        @pl.when(rank - step >= 0)
        def _(step=step):
            back_copy(step).wait_send()

    own_sends(lambda copy: copy.wait_send())

    def drain(step, carried):
        below = place - step
        above = place + step
        for piece in piece_ids:

            @pl.when(below >= 0)
            def _(piece=piece):
                chunk = below * 2 + side

                @pl.when(place + 1 < chain)
                def _():
                    w_copy(0, chunk, piece).wait_send()

                w_copy(2, chunk, piece).wait_send()

            @pl.when(above < chain)
            def _(piece=piece):
                chunk = above * 2 + side

                @pl.when(place >= 1)
                def _():
                    w_copy(1, chunk, piece).wait_send()

                w_copy(2, chunk, piece).wait_send()

        return carried

    loop(1, chain, drain, 0)
    for way in range(3):
        g_copy(way).wait_send()
    for target in (mate, across, diagonal):
        term_copy(target).wait_send()


def per_device(n_ctx, n_head, queries, key_states, value_states, doc_lengths, out_weight, out_grad):
    rows, q_cols = queries.shape
    heads = q_cols // HEAD_DIM
    wide = heads * rows
    w_rows = out_weight.shape[0]
    cols = out_grad.shape[1]
    blocks = REACH + 1
    pieces = ((0, w_rows // 2), (w_rows // 2, w_rows // 2))
    vmem = pl.BlockSpec(memory_space=pltpu.VMEM)
    hbm = pl.BlockSpec(memory_space=pl.ANY)
    dma = pltpu.SemaphoreType.DMA
    count = len(pieces)
    return pl.pallas_call(
        functools.partial(kernel, n_ctx, n_head, pieces),
        out_shape=(
            jax.ShapeDtypeStruct(out_grad.shape, BF16),
            jax.ShapeDtypeStruct(queries.shape, BF16),
            jax.ShapeDtypeStruct(key_states.shape, BF16),
            jax.ShapeDtypeStruct(value_states.shape, BF16),
        ),
        in_specs=[pl.BlockSpec(memory_space=pltpu.SMEM), vmem, vmem, vmem, hbm, hbm],
        out_specs=(vmem,) * 4,
        scratch_shapes=[
            pltpu.VMEM((2, blocks, rows, HEAD_DIM), BF16),
            pltpu.VMEM((2, blocks, HEAD_DIM, rows), BF16),
            pltpu.VMEM((wide, HEAD_DIM), BF16),
            pltpu.VMEM((blocks, rows, wide), F32),
            pltpu.VMEM((blocks, rows, wide), BF16),
            pltpu.VMEM((rows, q_cols), BF16),
            pltpu.VMEM((HEAD_DIM, wide), BF16),
            pltpu.VMEM((n_ctx * w_rows, q_cols), BF16),
            pltpu.VMEM((n_head, rows, cols), BF16),
            pltpu.VMEM((rows, q_cols), F32),
            pltpu.VMEM((wide, HEAD_DIM), BF16),
            pltpu.VMEM((HEAD_DIM, wide), BF16),
            pltpu.VMEM((1, wide), F32),
            pltpu.VMEM((rows, wide), BF16),
            pltpu.VMEM((HEAD_DIM, wide), F32),
            pltpu.VMEM((n_head, rows, cols), BF16),
            pltpu.VMEM((n_head, rows, cols), BF16),
            pltpu.VMEM((blocks, 2, rows, HEAD_DIM), BF16),
            pltpu.VMEM((blocks, 2, rows, HEAD_DIM), BF16),
            pltpu.VMEM((2, rows, HEAD_DIM), F32),
            dma((2, blocks)),
            dma((2, blocks)),
            dma((3, count, n_ctx)),
            dma((count, n_ctx)),
            dma,
            dma((3,)),
            dma((n_head,)),
            dma,
            dma((n_head,)),
            dma((n_head,)),
            dma((blocks,)),
            dma((blocks,)),
        ],
        compiler_params=pltpu.CompilerParams(
            collective_id=0, has_side_effects=True, vmem_limit_bytes=48 * 1024 * 1024
        ),
    )(doc_lengths, queries, key_states, value_states, out_weight, out_grad)


def solution(mesh):
    whole = P("ctx", "head")
    return jax.shard_map(
        functools.partial(per_device, mesh.shape["ctx"], mesh.shape["head"]),
        mesh=mesh,
        in_specs=(whole, whole, whole, P(), whole, whole),
        out_specs=(whole,) * 4,
        check_vma=False,
    )
```

```python
import functools

import jax
import jax.numpy as jnp
from jax import lax
from jax.experimental import pallas as pl
from jax.experimental.pallas import tpu as pltpu
from jax.sharding import PartitionSpec as P

HEAD_DIM = 128
REACH = 4
TILE = 256
NEGATIVE = -1e30
MESH = pl.DeviceIdType.MESH
F32 = jnp.float32
BF16 = jnp.bfloat16


def dot_nn(left, right):
    return jnp.dot(left, right, preferred_element_type=F32)


def dot_nt(left, right):
    return lax.dot_general(left, right, (((1,), (1,)), ((), ())), preferred_element_type=F32)


def loop(first, last, body, carried):
    if last - first > 8:
        return lax.fori_loop(first, last, body, carried)
    for index in range(first, last):
        carried = body(index, carried)
    return carried


def flip(value):
    return value.astype(F32).T.astype(BF16)


def kernel(
    n_ctx, n_head, pieces,
    doc_ref, q_ref, k_ref, v_ref, w_ref, g_ref,
    proj_ref, qg_ref, kg_ref, vg_ref,
    kv, kv_t, q_st, probs, probs_b, att, att_t, w_all, g_all, d_acc, d_st,
    delta, ds_b, dq_t, term, term_in, kv_out, kv_in, kv_acc,
    kv_send, kv_recv, w_send, w_recv, w_own, g_send, g_recv, g_own, t_send, t_recv, b_send, b_recv,
):
    rows = q_ref.shape[0]
    heads = q_ref.shape[1] // HEAD_DIM
    w_rows = w_ref.shape[0]
    cols = g_ref.shape[1]
    chain = n_ctx // 2
    tiles, tile = term_in.shape[1], term_in.shape[3]
    scale = HEAD_DIM ** (-0.5)
    rank = lax.axis_index("ctx")
    mine = lax.axis_index("head")
    place = rank // 2
    side = rank % 2
    other = 1 - side
    core = mine % 2
    half = mine // 2
    mate = half * 2 + (1 - core)
    across = (1 - half) * 2 + core
    diagonal = (1 - half) * 2 + (1 - core)

    barrier = pltpu.get_barrier_semaphore()
    for target in (mate, across, diagonal):
        pl.semaphore_signal(barrier, inc=1, device_id=(rank, target), device_id_type=MESH)
    for step in range(1, REACH + 1):

        @pl.when(rank - step >= 0)
        def _(step=step):
            pl.semaphore_signal(barrier, inc=1, device_id=(rank - step, mine), device_id_type=MESH)

        @pl.when(rank + step < n_ctx)
        def _(step=step):
            pl.semaphore_signal(barrier, inc=1, device_id=(rank + step, mine), device_id_type=MESH)

    below_me = jnp.where(rank < REACH, rank, REACH)
    above_me = jnp.where(n_ctx - 1 - rank < REACH, n_ctx - 1 - rank, REACH)
    pl.semaphore_wait(barrier, n_head - 1 + below_me + above_me)

    def kv_copy(step, which):
        return pltpu.make_async_remote_copy(
            src_ref=(k_ref, v_ref)[which],
            dst_ref=kv.at[which, step],
            send_sem=kv_send.at[which, step],
            recv_sem=kv_recv.at[which, step],
            device_id=(rank + step, mine),
            device_id_type=MESH,
        )

    def w_slot(chunk, piece):
        first, count = pieces[piece]
        return w_all.at[pl.ds(pl.multiple_of(chunk * w_rows + first, 16), count), :]

    def w_copy(way, chunk, piece, own=False):
        first, count = pieces[piece]
        target = (rank + 2, rank - 2, place * 2 + other)[way]
        return pltpu.make_async_remote_copy(
            src_ref=w_ref.at[pl.ds(first, count), :] if own else w_slot(chunk, piece),
            dst_ref=w_slot(chunk, piece),
            send_sem=w_send.at[way, piece, chunk],
            recv_sem=w_recv.at[piece, chunk],
            device_id=(target, mine),
            device_id_type=MESH,
        )

    def g_copy(way):
        source, target = ((mine, mate), (mine, across), (across, mate))[way]
        return pltpu.make_async_remote_copy(
            src_ref=g_all.at[source] if way == 2 else g_ref,
            dst_ref=g_all.at[source],
            send_sem=g_send.at[way],
            recv_sem=g_recv.at[source],
            device_id=(rank, target),
            device_id_type=MESH,
        )

    def g_arrival(source):
        return pltpu.make_async_remote_copy(
            src_ref=g_ref,
            dst_ref=g_all.at[source],
            send_sem=g_send.at[0],
            recv_sem=g_recv.at[source],
            device_id=(rank, mate),
            device_id_type=MESH,
        )

    def term_copy(index):
        return pltpu.make_async_remote_copy(
            src_ref=term.at[index],
            dst_ref=term_in.at[mine, index % tiles],
            send_sem=t_send.at[index],
            recv_sem=t_recv.at[mine, index % tiles],
            device_id=(rank, index // tiles),
            device_id_type=MESH,
        )

    def term_arrival(source, index):
        return pltpu.make_async_remote_copy(
            src_ref=term.at[index],
            dst_ref=term_in.at[source, index],
            send_sem=t_send.at[index],
            recv_sem=t_recv.at[source, index],
            device_id=(rank, mate),
            device_id_type=MESH,
        )

    def back_copy(step):
        return pltpu.make_async_remote_copy(
            src_ref=kv_out.at[step],
            dst_ref=kv_in.at[step],
            send_sem=b_send.at[step],
            recv_sem=b_recv.at[step],
            device_id=(rank - step, mine),
            device_id_type=MESH,
        )

    piece_ids = range(len(pieces))

    def own_sends(act):
        for piece in piece_ids:

            @pl.when(place + 1 < chain)
            def _(piece=piece):
                act(w_copy(0, rank, piece, own=True))

            @pl.when(place >= 1)
            def _(piece=piece):
                act(w_copy(1, rank, piece, own=True))

            act(w_copy(2, rank, piece, own=True))

    for step in range(1, REACH + 1):

        @pl.when(rank + step < n_ctx)
        def _(step=step):
            kv_copy(step, 0).start()
            kv_copy(step, 1).start()

    own_sends(lambda copy: copy.start())
    g_copy(1).start()
    g_copy(0).start()
    own_rows = w_all.at[pl.ds(pl.multiple_of(rank * w_rows, 16), w_rows), :]
    w_local = pltpu.make_async_copy(w_ref, own_rows, w_own)
    w_local.start()
    g_local = pltpu.make_async_copy(g_ref, g_all.at[mine], g_own)
    g_local.start()

    lanes = [pl.ds(head * rows, rows) for head in range(heads)]
    for head in range(heads):
        q_st[lanes[head], :] = q_ref[:, head * HEAD_DIM:(head + 1) * HEAD_DIM]
    kv[0, 0] = k_ref[...]
    kv[1, 0] = v_ref[...]

    positions = rank * rows + lax.broadcasted_iota(jnp.int32, (1, rows), 1)

    def add_doc(index, carried):
        end, starts = carried
        length = doc_ref[index]
        end = end + length
        return end, starts + jnp.where(end <= positions, length, 0)

    _, starts = loop(
        0, doc_ref.shape[0], add_doc, (jnp.int32(0), jnp.zeros((1, rows), jnp.int32))
    )

    def score_block(step, maxima):
        @pl.when(jnp.logical_and(step > 0, rank - step >= 0))
        def _():
            for which in range(2):
                pltpu.make_async_remote_copy(
                    src_ref=(k_ref, v_ref)[which],
                    dst_ref=kv.at[which, step],
                    send_sem=kv_send.at[which, step],
                    recv_sem=kv_recv.at[which, step],
                    device_id=(rank, mate),
                    device_id_type=MESH,
                ).wait_recv()

        @pl.when(rank - step < 0)
        def _():
            kv[0, step] = jnp.zeros((rows, HEAD_DIM), BF16)
            kv[1, step] = jnp.zeros((rows, HEAD_DIM), BF16)

        key_block = kv[0, step]
        kv_t[0, step] = flip(key_block)
        kv_t[1, step] = flip(kv[1, step])
        key_pos = (rank - step) * rows + lax.broadcasted_iota(jnp.int32, (rows, rows), 0)
        allowed = jnp.logical_and(key_pos >= starts, key_pos <= positions)
        result = []
        for head in range(heads):
            scores = dot_nt(key_block, q_st[lanes[head], :]) * scale
            scores = jnp.where(allowed, scores, NEGATIVE)
            probs[step, :, lanes[head]] = scores
            result.append(jnp.maximum(maxima[head], jnp.max(scores, axis=0, keepdims=True)))
        return tuple(result)

    low = jnp.full((1, rows), NEGATIVE, F32)
    maxima = loop(0, REACH + 1, score_block, (low,) * heads)

    def exp_block(step, sums):
        result = []
        for head in range(heads):
            powers = jnp.exp(probs[step, :, lanes[head]] - maxima[head])
            probs[step, :, lanes[head]] = powers
            result.append(sums[head] + jnp.sum(powers, axis=0, keepdims=True))
        return tuple(result)

    zero = jnp.zeros((1, rows), F32)
    sums = loop(0, REACH + 1, exp_block, (zero,) * heads)
    inverses = [1.0 / total for total in sums]
    dq_t[...] = jnp.zeros_like(dq_t)

    def relays(step):
        below = place - step
        above = place + step
        for piece in piece_ids:

            @pl.when(below >= 0)
            def _(piece=piece):
                chunk = below * 2 + side
                w_copy(0, chunk, piece).wait_recv()

                @pl.when(place + 1 < chain)
                def _():
                    w_copy(0, chunk, piece).start()

                w_copy(2, chunk, piece).start()

            @pl.when(above < chain)
            def _(piece=piece):
                chunk = above * 2 + side
                w_copy(1, chunk, piece).wait_recv()

                @pl.when(place >= 1)
                def _():
                    w_copy(1, chunk, piece).start()

                w_copy(2, chunk, piece).start()

    relays(1)

    def mix_block(step, carried):
        for head in range(heads):
            exact = probs[step, :, lanes[head]] * inverses[head]
            probs[step, :, lanes[head]] = exact
            probs_b[step, :, lanes[head]] = exact.astype(BF16)
        dq_t[...] += dot_nn(kv_t[1, step], probs_b[step])
        return carried

    loop(0, REACH + 1, mix_block, 0)
    for head in range(heads):
        mixed = dq_t[:, lanes[head]]
        att_t[:, lanes[head]] = mixed.astype(BF16)
        att[:, head * HEAD_DIM:(head + 1) * HEAD_DIM] = mixed.T.astype(BF16)

    w_local.wait()
    g_local.wait()
    g_arrival(across).wait_recv()
    g_copy(2).start()
    g_arrival(mate).wait_recv()
    g_arrival(diagonal).wait_recv()
    d_acc[...] = jnp.zeros_like(d_acc)

    def process(index):
        w_tile = w_all[pl.ds(pl.multiple_of(index * tile, tile), tile), :]
        first = pl.multiple_of(index % tiles * tile, tile)
        d_acc[...] += dot_nn(g_all[index // tiles, :, pl.ds(first, tile)], w_tile)
        term[index] = dot_nt(att[...], w_tile).astype(BF16)

        @pl.when(index // tiles != mine)
        def _():
            term_copy(index).start()

    early = w_rows == len(pieces) * tile

    def count_of(step):
        return 1 if isinstance(step, int) and step == 0 else 2

    def finish(step):
        for piece in piece_ids:
            for spot in (place - step, place + step)[:count_of(step)]:

                @pl.when(jnp.logical_and(spot >= 0, spot < chain))
                def _(piece=piece, spot=spot):
                    chunk = spot * 2 + other
                    w_copy(2, chunk, piece).wait_recv()
                    if early:
                        process(chunk * len(pieces) + piece)

    def direct(step):
        if early:
            for piece in piece_ids:
                for spot in (place - step, place + step)[:count_of(step)]:

                    @pl.when(jnp.logical_and(spot >= 0, spot < chain))
                    def _(piece=piece, spot=spot):
                        process((spot * 2 + side) * len(pieces) + piece)

    def later(step, carried):
        relays(step)
        finish(step - 1)
        direct(step)
        return carried

    direct(0)
    finish(0)
    direct(1)
    loop(2, chain, later, 0)
    finish(chain - 1)
    if not early:

        def late(index, carried):
            process(index)
            return carried

        loop(0, n_head * tiles, late, 0)

    for head in range(heads):
        part = d_acc[:, head * HEAD_DIM:(head + 1) * HEAD_DIM].astype(BF16)
        d_st[lanes[head], :] = part
        turned = part.astype(F32).T
        delta[:, lanes[head]] = jnp.sum(
            turned * att_t[:, lanes[head]].astype(F32), axis=0, keepdims=True
        )
    dq_t[...] = jnp.zeros_like(dq_t)

    def grad_block(index, carried):
        step = REACH - index
        value_block = kv[1, step]
        for head in range(heads):
            d_probs = dot_nt(value_block, d_st[lanes[head], :])
            d_scores = probs[step, :, lanes[head]] * (d_probs - delta[:, lanes[head]])
            ds_b[:, lanes[head]] = d_scores.astype(BF16)
        key_part = dot_nn(ds_b[...], q_st[...])
        value_part = dot_nn(probs_b[step], d_st[...])

        @pl.when(step == 0)
        def _():
            kv_acc[0] = key_part
            kv_acc[1] = value_part

        @pl.when(jnp.logical_and(step > 0, rank - step >= 0))
        def _():
            kv_out[step, 0] = key_part.astype(BF16)
            kv_out[step, 1] = value_part.astype(BF16)
            back_copy(step).start()

        dq_t[...] += dot_nn(kv_t[0, step], ds_b[...])
        return carried

    loop(0, REACH + 1, grad_block, 0)
    for head in range(heads):
        qg_ref[:, head * HEAD_DIM:(head + 1) * HEAD_DIM] = (
            (dq_t[:, lanes[head]] * scale).T.astype(BF16)
        )

    for index in range(tiles):
        summed = term[mine * tiles + index].astype(F32)
        for source in (mate, across, diagonal):
            term_arrival(source, index).wait_recv()
            summed = summed + term_in[source, index].astype(F32)
        proj_ref[:, index * tile:(index + 1) * tile] = summed.astype(BF16)

    for step in range(REACH, 0, -1):

        @pl.when(rank + step < n_ctx)
        def _(step=step):
            back_copy(step).wait_recv()
            kv_acc[...] += kv_in[step].astype(F32)

    kg_ref[...] = (kv_acc[0] * scale).astype(BF16)
    vg_ref[...] = kv_acc[1].astype(BF16)

    for step in range(1, REACH + 1):

        @pl.when(rank + step < n_ctx)
        def _(step=step):
            kv_copy(step, 0).wait_send()
            kv_copy(step, 1).wait_send()

        @pl.when(rank - step >= 0)
        def _(step=step):
            back_copy(step).wait_send()

    own_sends(lambda copy: copy.wait_send())

    def drain(step, carried):
        below = place - step
        above = place + step
        for piece in piece_ids:

            @pl.when(below >= 0)
            def _(piece=piece):
                chunk = below * 2 + side

                @pl.when(place + 1 < chain)
                def _():
                    w_copy(0, chunk, piece).wait_send()

                w_copy(2, chunk, piece).wait_send()

            @pl.when(above < chain)
            def _(piece=piece):
                chunk = above * 2 + side

                @pl.when(place >= 1)
                def _():
                    w_copy(1, chunk, piece).wait_send()

                w_copy(2, chunk, piece).wait_send()

        return carried

    loop(1, chain, drain, 0)
    for way in range(3):
        g_copy(way).wait_send()
    for index in range(n_head * tiles):

        @pl.when(mine != index // tiles)
        def _(index=index):
            term_copy(index).wait_send()


def per_device(n_ctx, n_head, queries, key_states, value_states, doc_lengths, out_weight, out_grad):
    rows, q_cols = queries.shape
    heads = q_cols // HEAD_DIM
    wide = heads * rows
    w_rows = out_weight.shape[0]
    cols = out_grad.shape[1]
    blocks = REACH + 1
    tile = min(TILE, cols)
    tiles = cols // tile
    pieces = ((0, w_rows // 2), (w_rows // 2, w_rows // 2))
    vmem = pl.BlockSpec(memory_space=pltpu.VMEM)
    hbm = pl.BlockSpec(memory_space=pl.ANY)
    dma = pltpu.SemaphoreType.DMA
    count = len(pieces)
    return pl.pallas_call(
        functools.partial(kernel, n_ctx, n_head, pieces),
        out_shape=(
            jax.ShapeDtypeStruct(out_grad.shape, BF16),
            jax.ShapeDtypeStruct(queries.shape, BF16),
            jax.ShapeDtypeStruct(key_states.shape, BF16),
            jax.ShapeDtypeStruct(value_states.shape, BF16),
        ),
        in_specs=[pl.BlockSpec(memory_space=pltpu.SMEM), vmem, vmem, vmem, hbm, hbm],
        out_specs=(vmem,) * 4,
        scratch_shapes=[
            pltpu.VMEM((2, blocks, rows, HEAD_DIM), BF16),
            pltpu.VMEM((2, blocks, HEAD_DIM, rows), BF16),
            pltpu.VMEM((wide, HEAD_DIM), BF16),
            pltpu.VMEM((blocks, rows, wide), F32),
            pltpu.VMEM((blocks, rows, wide), BF16),
            pltpu.VMEM((rows, q_cols), BF16),
            pltpu.VMEM((HEAD_DIM, wide), BF16),
            pltpu.VMEM((n_ctx * w_rows, q_cols), BF16),
            pltpu.VMEM((n_head, rows, cols), BF16),
            pltpu.VMEM((rows, q_cols), F32),
            pltpu.VMEM((wide, HEAD_DIM), BF16),
            pltpu.VMEM((1, wide), F32),
            pltpu.VMEM((rows, wide), BF16),
            pltpu.VMEM((HEAD_DIM, wide), F32),
            pltpu.VMEM((n_head * tiles, rows, tile), BF16),
            pltpu.VMEM((n_head, tiles, rows, tile), BF16),
            pltpu.VMEM((blocks, 2, rows, HEAD_DIM), BF16),
            pltpu.VMEM((blocks, 2, rows, HEAD_DIM), BF16),
            pltpu.VMEM((2, rows, HEAD_DIM), F32),
            dma((2, blocks)),
            dma((2, blocks)),
            dma((3, count, n_ctx)),
            dma((count, n_ctx)),
            dma,
            dma((3,)),
            dma((n_head,)),
            dma,
            dma((n_head * tiles,)),
            dma((n_head, tiles)),
            dma((blocks,)),
            dma((blocks,)),
        ],
        compiler_params=pltpu.CompilerParams(
            collective_id=0, has_side_effects=True, vmem_limit_bytes=60 * 1024 * 1024
        ),
    )(doc_lengths, queries, key_states, value_states, out_weight, out_grad)


def solution(mesh):
    whole = P("ctx", "head")
    return jax.shard_map(
        functools.partial(per_device, mesh.shape["ctx"], mesh.shape["head"]),
        mesh=mesh,
        in_specs=(whole, whole, whole, P(), whole, whole),
        out_specs=(whole,) * 4,
        check_vma=False,
    )
```

```python
import functools

import jax
import jax.numpy as jnp
from jax import lax
from jax.experimental import pallas as pl
from jax.experimental.pallas import tpu as pltpu
from jax.sharding import PartitionSpec as P

HEAD_DIM = 128
REACH = 4
TILE = 256
NEGATIVE = -1e30
MESH = pl.DeviceIdType.MESH
F32 = jnp.float32
BF16 = jnp.bfloat16


def dot_nn(left, right):
    return jnp.dot(left, right, preferred_element_type=F32)


def dot_nt(left, right):
    return lax.dot_general(left, right, (((1,), (1,)), ((), ())), preferred_element_type=F32)


def loop(first, last, body, carried):
    if last - first > 8:
        return lax.fori_loop(first, last, body, carried)
    for index in range(first, last):
        carried = body(index, carried)
    return carried


def flip(value):
    return value.astype(F32).T.astype(BF16)


def kernel(
    n_ctx, n_head, pieces,
    doc_ref, q_ref, k_ref, v_ref, w_ref, g_ref,
    proj_ref, qg_ref, kg_ref, vg_ref,
    kv, kv_t, q_st, probs, probs_b, att, att_t, w_all, g_all, d_acc, d_st,
    delta, ds_b, dq_t, term, term_in, kv_out, kv_in, kv_acc,
    kv_send, kv_recv, w_send, w_recv, w_own, g_send, g_recv, g_own, t_send, t_recv, b_send, b_recv,
):
    rows = q_ref.shape[0]
    heads = q_ref.shape[1] // HEAD_DIM
    w_rows = w_ref.shape[0]
    cols = g_ref.shape[1]
    chain = n_ctx // 2
    tiles, tile = term_in.shape[1], term_in.shape[3]
    scale = HEAD_DIM ** (-0.5)
    rank = lax.axis_index("ctx")
    mine = lax.axis_index("head")
    place = rank // 2
    side = rank % 2
    other = 1 - side
    core = mine % 2
    half = mine // 2
    mate = half * 2 + (1 - core)
    across = (1 - half) * 2 + core
    diagonal = (1 - half) * 2 + (1 - core)

    kv[0, 0] = k_ref[...]
    kv[0, 1] = v_ref[...]
    barrier = pltpu.get_barrier_semaphore()
    for target in (mate, across, diagonal):
        pl.semaphore_signal(barrier, inc=1, device_id=(rank, target), device_id_type=MESH)
    for step in range(1, REACH + 1):

        @pl.when(rank - step >= 0)
        def _(step=step):
            pl.semaphore_signal(barrier, inc=1, device_id=(rank - step, mine), device_id_type=MESH)

        @pl.when(rank + step < n_ctx)
        def _(step=step):
            pl.semaphore_signal(barrier, inc=1, device_id=(rank + step, mine), device_id_type=MESH)

    below_me = jnp.where(rank < REACH, rank, REACH)
    above_me = jnp.where(n_ctx - 1 - rank < REACH, n_ctx - 1 - rank, REACH)
    pl.semaphore_wait(barrier, n_head - 1 + below_me + above_me)

    def kv_copy(way):
        source, slot, target = (
            (0, 1 + REACH * side, place * 2 + other),
            (0, 2, rank + 2),
            (0, 4, rank + 4),
            (1 + REACH * other, 1 + 2 * side, rank + 2),
            (1 + REACH, 3, rank + 4),
        )[way]
        return pltpu.make_async_remote_copy(
            src_ref=kv.at[source],
            dst_ref=kv.at[slot],
            send_sem=kv_send.at[way],
            recv_sem=kv_recv.at[slot],
            device_id=(target, mine),
            device_id_type=MESH,
        )

    def kv_arrival(slot):
        return pltpu.make_async_remote_copy(
            src_ref=kv.at[0],
            dst_ref=kv.at[slot],
            send_sem=kv_send.at[0],
            recv_sem=kv_recv.at[slot],
            device_id=(rank, mate),
            device_id_type=MESH,
        )

    def kv_sends(ways, act):
        for way in ways:
            needed = (
                place >= 0,
                place + 1 < chain,
                place + 2 < chain,
                place + 1 < chain,
                jnp.logical_and(place + 2 < chain, side == 0),
            )[way]

            @pl.when(needed)
            def _(way=way):
                act(kv_copy(way))

    def w_slot(chunk, piece):
        first, count = pieces[piece]
        return w_all.at[pl.ds(pl.multiple_of(chunk * w_rows + first, 16), count), :]

    def w_copy(way, chunk, piece, own=False):
        first, count = pieces[piece]
        target = (rank + 2, rank - 2, place * 2 + other)[way]
        return pltpu.make_async_remote_copy(
            src_ref=w_ref.at[pl.ds(first, count), :] if own else w_slot(chunk, piece),
            dst_ref=w_slot(chunk, piece),
            send_sem=w_send.at[way, piece, chunk],
            recv_sem=w_recv.at[piece, chunk],
            device_id=(target, mine),
            device_id_type=MESH,
        )

    def g_copy(way):
        source, target = ((mine, mate), (mine, across), (across, mate))[way]
        return pltpu.make_async_remote_copy(
            src_ref=g_all.at[source] if way == 2 else g_ref,
            dst_ref=g_all.at[source],
            send_sem=g_send.at[way],
            recv_sem=g_recv.at[source],
            device_id=(rank, target),
            device_id_type=MESH,
        )

    def g_arrival(source):
        return pltpu.make_async_remote_copy(
            src_ref=g_ref,
            dst_ref=g_all.at[source],
            send_sem=g_send.at[0],
            recv_sem=g_recv.at[source],
            device_id=(rank, mate),
            device_id_type=MESH,
        )

    def term_copy(index):
        return pltpu.make_async_remote_copy(
            src_ref=term.at[index],
            dst_ref=term_in.at[mine, index % tiles],
            send_sem=t_send.at[index],
            recv_sem=t_recv.at[mine, index % tiles],
            device_id=(rank, index // tiles),
            device_id_type=MESH,
        )

    def term_arrival(source, index):
        return pltpu.make_async_remote_copy(
            src_ref=term.at[index],
            dst_ref=term_in.at[source, index],
            send_sem=t_send.at[index],
            recv_sem=t_recv.at[source, index],
            device_id=(rank, mate),
            device_id_type=MESH,
        )

    def back_copy(step):
        return pltpu.make_async_remote_copy(
            src_ref=kv_out.at[step],
            dst_ref=kv_in.at[step],
            send_sem=b_send.at[step],
            recv_sem=b_recv.at[step],
            device_id=(rank - step, mine),
            device_id_type=MESH,
        )

    piece_ids = range(len(pieces))

    def start(copy):
        copy.start()

    def wait_send(copy):
        copy.wait_send()

    def own_sends(act):
        for piece in piece_ids:

            @pl.when(place >= 1)
            def _(piece=piece):
                act(w_copy(1, rank, piece, own=True))

            act(w_copy(2, rank, piece, own=True))

    def own_up(act):
        for piece in piece_ids:

            @pl.when(place + 1 < chain)
            def _(piece=piece):
                act(w_copy(0, rank, piece, own=True))

    kv_sends(range(3), start)
    own_sends(start)
    g_copy(1).start()
    g_copy(0).start()
    own_rows = w_all.at[pl.ds(pl.multiple_of(rank * w_rows, 16), w_rows), :]
    w_local = pltpu.make_async_copy(w_ref, own_rows, w_own)
    w_local.start()
    g_local = pltpu.make_async_copy(g_ref, g_all.at[mine], g_own)
    g_local.start()

    kv_arrival(1 + REACH * other).wait_recv()
    kv_sends(range(3, 5), start)
    own_up(start)

    lanes = [pl.ds(head * rows, rows) for head in range(heads)]
    for head in range(heads):
        q_st[lanes[head], :] = q_ref[:, head * HEAD_DIM:(head + 1) * HEAD_DIM]

    positions = rank * rows + lax.broadcasted_iota(jnp.int32, (1, rows), 1)

    def add_doc(index, carried):
        end, starts = carried
        length = doc_ref[index]
        end = end + length
        return end, starts + jnp.where(end <= positions, length, 0)

    _, starts = loop(
        0, doc_ref.shape[0], add_doc, (jnp.int32(0), jnp.zeros((1, rows), jnp.int32))
    )

    def score_block(step, maxima):
        if step > 0:

            @pl.when(jnp.logical_and(rank - step >= 0, jnp.logical_or(step > 1, side == 0)))
            def _():
                kv_arrival(step).wait_recv()

        @pl.when(rank - step < 0)
        def _():
            kv[step] = jnp.zeros((2, rows, HEAD_DIM), BF16)

        key_block = kv[step, 0]
        kv_t[0, step] = flip(key_block)
        kv_t[1, step] = flip(kv[step, 1])
        key_pos = (rank - step) * rows + lax.broadcasted_iota(jnp.int32, (rows, rows), 0)
        allowed = jnp.logical_and(key_pos >= starts, key_pos <= positions)
        result = []
        for head in range(heads):
            scores = dot_nt(key_block, q_st[lanes[head], :]) * scale
            scores = jnp.where(allowed, scores, NEGATIVE)
            probs[step, :, lanes[head]] = scores
            result.append(jnp.maximum(maxima[head], jnp.max(scores, axis=0, keepdims=True)))
        return tuple(result)

    low = jnp.full((1, rows), NEGATIVE, F32)
    maxima = loop(0, REACH + 1, score_block, (low,) * heads)

    def exp_block(step, sums):
        result = []
        for head in range(heads):
            powers = jnp.exp(probs[step, :, lanes[head]] - maxima[head])
            probs[step, :, lanes[head]] = powers
            result.append(sums[head] + jnp.sum(powers, axis=0, keepdims=True))
        return tuple(result)

    zero = jnp.zeros((1, rows), F32)
    sums = loop(0, REACH + 1, exp_block, (zero,) * heads)
    inverses = [1.0 / total for total in sums]
    dq_t[...] = jnp.zeros_like(dq_t)

    def relays(step):
        below = place - step
        above = place + step
        for piece in piece_ids:

            @pl.when(below >= 0)
            def _(piece=piece):
                chunk = below * 2 + side
                w_copy(0, chunk, piece).wait_recv()

                @pl.when(place + 1 < chain)
                def _():
                    w_copy(0, chunk, piece).start()

                w_copy(2, chunk, piece).start()

            @pl.when(above < chain)
            def _(piece=piece):
                chunk = above * 2 + side
                w_copy(1, chunk, piece).wait_recv()

                @pl.when(place >= 1)
                def _():
                    w_copy(1, chunk, piece).start()

                w_copy(2, chunk, piece).start()

    relays(1)

    def mix_block(step, carried):
        for head in range(heads):
            exact = probs[step, :, lanes[head]] * inverses[head]
            probs[step, :, lanes[head]] = exact
            probs_b[step, :, lanes[head]] = exact.astype(BF16)
        dq_t[...] += dot_nn(kv_t[1, step], probs_b[step])
        return carried

    loop(0, REACH + 1, mix_block, 0)
    for head in range(heads):
        mixed = dq_t[:, lanes[head]]
        att_t[:, lanes[head]] = mixed.astype(BF16)
        att[:, head * HEAD_DIM:(head + 1) * HEAD_DIM] = mixed.T.astype(BF16)

    w_local.wait()
    g_local.wait()
    g_arrival(across).wait_recv()
    g_copy(2).start()
    g_arrival(mate).wait_recv()
    g_arrival(diagonal).wait_recv()
    d_acc[...] = jnp.zeros_like(d_acc)

    def process(index):
        w_tile = w_all[pl.ds(pl.multiple_of(index * tile, tile), tile), :]
        first = pl.multiple_of(index % tiles * tile, tile)
        d_acc[...] += dot_nn(g_all[index // tiles, :, pl.ds(first, tile)], w_tile)
        term[index] = dot_nt(att[...], w_tile).astype(BF16)

        @pl.when(index // tiles != mine)
        def _():
            term_copy(index).start()

    early = w_rows == len(pieces) * tile

    def count_of(step):
        return 1 if isinstance(step, int) and step == 0 else 2

    def finish(step):
        for piece in piece_ids:
            for spot in (place - step, place + step)[:count_of(step)]:

                @pl.when(jnp.logical_and(spot >= 0, spot < chain))
                def _(piece=piece, spot=spot):
                    chunk = spot * 2 + other
                    w_copy(2, chunk, piece).wait_recv()
                    if early:
                        process(chunk * len(pieces) + piece)

    def direct(step):
        if early:
            for piece in piece_ids:
                for spot in (place - step, place + step)[:count_of(step)]:

                    @pl.when(jnp.logical_and(spot >= 0, spot < chain))
                    def _(piece=piece, spot=spot):
                        process((spot * 2 + side) * len(pieces) + piece)

    def later(step, carried):
        relays(step)
        finish(step - 1)
        direct(step)
        return carried

    direct(0)
    finish(0)
    direct(1)
    loop(2, chain, later, 0)
    finish(chain - 1)
    if not early:

        def late(index, carried):
            process(index)
            return carried

        loop(0, n_head * tiles, late, 0)

    for head in range(heads):
        part = d_acc[:, head * HEAD_DIM:(head + 1) * HEAD_DIM].astype(BF16)
        d_st[lanes[head], :] = part
        turned = part.astype(F32).T
        delta[:, lanes[head]] = jnp.sum(
            turned * att_t[:, lanes[head]].astype(F32), axis=0, keepdims=True
        )
    dq_t[...] = jnp.zeros_like(dq_t)

    def grad_block(index, carried):
        step = REACH - index
        value_block = kv[step, 1]
        for head in range(heads):
            d_probs = dot_nt(value_block, d_st[lanes[head], :])
            d_scores = probs[step, :, lanes[head]] * (d_probs - delta[:, lanes[head]])
            ds_b[:, lanes[head]] = d_scores.astype(BF16)
        key_part = dot_nn(ds_b[...], q_st[...])
        value_part = dot_nn(probs_b[step], d_st[...])

        @pl.when(step == 0)
        def _():
            kv_acc[0] = key_part
            kv_acc[1] = value_part

        @pl.when(jnp.logical_and(step > 0, rank - step >= 0))
        def _():
            kv_out[step, 0] = key_part.astype(BF16)
            kv_out[step, 1] = value_part.astype(BF16)
            back_copy(step).start()

        dq_t[...] += dot_nn(kv_t[0, step], ds_b[...])
        return carried

    loop(0, REACH + 1, grad_block, 0)
    for head in range(heads):
        qg_ref[:, head * HEAD_DIM:(head + 1) * HEAD_DIM] = (
            (dq_t[:, lanes[head]] * scale).T.astype(BF16)
        )

    for index in range(tiles):
        summed = term[mine * tiles + index].astype(F32)
        for source in (mate, across, diagonal):
            term_arrival(source, index).wait_recv()
            summed = summed + term_in[source, index].astype(F32)
        proj_ref[:, index * tile:(index + 1) * tile] = summed.astype(BF16)

    for step in range(REACH, 0, -1):

        @pl.when(rank + step < n_ctx)
        def _(step=step):
            back_copy(step).wait_recv()
            kv_acc[...] += kv_in[step].astype(F32)

    kg_ref[...] = (kv_acc[0] * scale).astype(BF16)
    vg_ref[...] = kv_acc[1].astype(BF16)

    for step in range(1, REACH + 1):

        @pl.when(rank - step >= 0)
        def _(step=step):
            back_copy(step).wait_send()

    own_sends(wait_send)
    own_up(wait_send)
    kv_sends(range(5), wait_send)

    def drain(step, carried):
        below = place - step
        above = place + step
        for piece in piece_ids:

            @pl.when(below >= 0)
            def _(piece=piece):
                chunk = below * 2 + side

                @pl.when(place + 1 < chain)
                def _():
                    w_copy(0, chunk, piece).wait_send()

                w_copy(2, chunk, piece).wait_send()

            @pl.when(above < chain)
            def _(piece=piece):
                chunk = above * 2 + side

                @pl.when(place >= 1)
                def _():
                    w_copy(1, chunk, piece).wait_send()

                w_copy(2, chunk, piece).wait_send()

        return carried

    loop(1, chain, drain, 0)
    for way in range(3):
        g_copy(way).wait_send()
    for index in range(n_head * tiles):

        @pl.when(mine != index // tiles)
        def _(index=index):
            term_copy(index).wait_send()


def per_device(n_ctx, n_head, queries, key_states, value_states, doc_lengths, out_weight, out_grad):
    rows, q_cols = queries.shape
    heads = q_cols // HEAD_DIM
    wide = heads * rows
    w_rows = out_weight.shape[0]
    cols = out_grad.shape[1]
    blocks = REACH + 1
    tile = min(TILE, cols)
    tiles = cols // tile
    pieces = ((0, w_rows // 2), (w_rows // 2, w_rows // 2))
    vmem = pl.BlockSpec(memory_space=pltpu.VMEM)
    hbm = pl.BlockSpec(memory_space=pl.ANY)
    dma = pltpu.SemaphoreType.DMA
    count = len(pieces)
    return pl.pallas_call(
        functools.partial(kernel, n_ctx, n_head, pieces),
        out_shape=(
            jax.ShapeDtypeStruct(out_grad.shape, BF16),
            jax.ShapeDtypeStruct(queries.shape, BF16),
            jax.ShapeDtypeStruct(key_states.shape, BF16),
            jax.ShapeDtypeStruct(value_states.shape, BF16),
        ),
        in_specs=[pl.BlockSpec(memory_space=pltpu.SMEM), vmem, vmem, vmem, hbm, hbm],
        out_specs=(vmem,) * 4,
        scratch_shapes=[
            pltpu.VMEM((blocks + 1, 2, rows, HEAD_DIM), BF16),
            pltpu.VMEM((2, blocks, HEAD_DIM, rows), BF16),
            pltpu.VMEM((wide, HEAD_DIM), BF16),
            pltpu.VMEM((blocks, rows, wide), F32),
            pltpu.VMEM((blocks, rows, wide), BF16),
            pltpu.VMEM((rows, q_cols), BF16),
            pltpu.VMEM((HEAD_DIM, wide), BF16),
            pltpu.VMEM((n_ctx * w_rows, q_cols), BF16),
            pltpu.VMEM((n_head, rows, cols), BF16),
            pltpu.VMEM((rows, q_cols), F32),
            pltpu.VMEM((wide, HEAD_DIM), BF16),
            pltpu.VMEM((1, wide), F32),
            pltpu.VMEM((rows, wide), BF16),
            pltpu.VMEM((HEAD_DIM, wide), F32),
            pltpu.VMEM((n_head * tiles, rows, tile), BF16),
            pltpu.VMEM((n_head, tiles, rows, tile), BF16),
            pltpu.VMEM((blocks, 2, rows, HEAD_DIM), BF16),
            pltpu.VMEM((blocks, 2, rows, HEAD_DIM), BF16),
            pltpu.VMEM((2, rows, HEAD_DIM), F32),
            dma((blocks,)),
            dma((blocks + 1,)),
            dma((3, count, n_ctx)),
            dma((count, n_ctx)),
            dma,
            dma((3,)),
            dma((n_head,)),
            dma,
            dma((n_head * tiles,)),
            dma((n_head, tiles)),
            dma((blocks,)),
            dma((blocks,)),
        ],
        compiler_params=pltpu.CompilerParams(
            collective_id=0, has_side_effects=True, vmem_limit_bytes=60 * 1024 * 1024
        ),
    )(doc_lengths, queries, key_states, value_states, out_weight, out_grad)


def solution(mesh):
    whole = P("ctx", "head")
    return jax.shard_map(
        functools.partial(per_device, mesh.shape["ctx"], mesh.shape["head"]),
        mesh=mesh,
        in_specs=(whole, whole, whole, P(), whole, whole),
        out_specs=(whole,) * 4,
        check_vma=False,
    )
```
